32 devices in a mesh: rows: 32 (over z, y, x, core), sub: 1.
Axes of the slice: x: 2, y: 2, z: 4, core: 2. Of those that a mesh axis runs over, the one named last changes fastest.
Arguments:
- embeddings: bfloat16 [16384, 1024], P('rows', 'sub'), may hold values from -40 to 40
- rotation: bfloat16 [1024, 1024], P(None, 'sub'), may hold values from -0.1875 to 0.1875
- codebooks: float32 [64, 16, 256], P('sub'), may hold values from -6 to 6
Outputs:
- new_codebooks: float32 [64, 16, 256], P('sub')
- new_rotation: float32 [1024, 1024], P('rows', 'sub')
The draws below stay inside these ranges and needn't reach their ends.
All inputs are finite; a program needn't handle non-finite values.
Results may differ from the reference program's by a relative error of at most 0.006.
The reference program's roundings to bfloat16 on the way count: a program that leaves them out, or rounds other values in their place, can miss the bound.
Values may be sent and summed in bfloat16 or wider, within the bound.
A program may use at most 64 MiB of HBM per device.

```python
import jax
import jax.numpy as jnp
from jax import lax

D = 1024
SUBS = 64
CODES = 256
SUB_DIM = 16
ROW_DEV = 512
ITERS = 2
POLAR_ITER_COUNT = 2
ROWS = 16384
N_ROWS = 32


def draw_embeddings(key, part):
    base_key = jax.random.fold_in(key, 11)
    values = jax.random.normal(jax.random.fold_in(base_key, 1), (ROWS, D), jnp.float32)
    scale_key = jax.random.fold_in(base_key, 2)
    scales = jnp.exp(jax.random.uniform(scale_key, (ROWS, 1), jnp.float32, -1.2, 1.2))
    values = values * scales
    return jnp.clip(values, -40.0, 40.0).astype(jnp.bfloat16)


def gaussian(key, extent, scale, reach, kind=jnp.bfloat16):
    return jnp.clip(scale * jax.random.normal(key, extent, jnp.float32), -reach, reach).astype(kind)


def setup_inputs(seed: int = 0) -> dict:
    streams_of = jax.random.split(jax.random.key(seed), 4)
    return {
        "embeddings": draw_embeddings(jax.random.fold_in(streams_of[3], 71), 0),
        "rotation": gaussian(streams_of[1], (D, D), D ** -0.5, 0.1875),
        "codebooks": gaussian(streams_of[2], (SUBS, SUB_DIM, CODES), 1.0, 6.0, jnp.float32),
    }


softness_level = 4.0
prior_weight = 8.0
quintic_one = 3.4445
quintic_three = -4.775
quintic_five = 2.0315

def soft_weights(row_block, centroid_tables):
    pieces = row_block.reshape(row_block.shape[0], SUBS, SUB_DIM).astype(jnp.float32)
    codes_low = lax.optimization_barrier(centroid_tables.astype(jnp.bfloat16)).astype(jnp.float32)
    cross_products = jnp.einsum('bmd,mdk->bmk', pieces, codes_low)
    centroid_logits = (2.0 * cross_products - lax.optimization_barrier(jnp.sum(centroid_tables * centroid_tables, axis=1))[None]) / softness_level
    return jax.nn.softmax(centroid_logits, axis=-1).astype(jnp.bfloat16)

def reference(embeddings, rotation, codebooks):
    rotated = jnp.dot(embeddings, rotation, preferred_element_type=jnp.float32).astype(jnp.bfloat16)
    row_blocks = rotated.reshape(N_ROWS, ROW_DEV, D)
    books_now = codebooks
    books_prev = codebooks
    for repeat in range(ITERS):

        def gather_stats(running, row_block):
            weights = soft_weights(row_block, books_now).astype(jnp.float32)
            pieces = row_block.reshape(ROW_DEV, SUBS, SUB_DIM).astype(jnp.float32)
            return ((running[0] + lax.optimization_barrier(jnp.sum(weights, axis=0)), running[1] + jnp.einsum('bmd,bmk->mdk', pieces, weights)), None)
        start_vals = (jnp.zeros((SUBS, CODES), jnp.float32), jnp.zeros((SUBS, SUB_DIM, CODES), jnp.float32))
        (counts, totals), _ = lax.scan(gather_stats, start_vals, row_blocks)
        books_prev = books_now
        books_now = (totals + prior_weight * books_now) / (counts[:, None, :] + prior_weight)
    codes_low = lax.optimization_barrier(books_now.astype(jnp.bfloat16)).astype(jnp.float32)
    x_blocks = embeddings.reshape(N_ROWS, ROW_DEV, D)

    def add_cross(running, paired):
        row_block, x_block = paired
        weights = soft_weights(row_block, books_prev).astype(jnp.float32)
        rebuilt = jnp.einsum('bmk,mdk->bmd', weights, codes_low).reshape(ROW_DEV, D).astype(jnp.bfloat16)
        return (running + jnp.dot(x_block.T, rebuilt, preferred_element_type=jnp.float32), None)
    cross_products, _ = lax.scan(add_cross, jnp.zeros((D, D), jnp.float32), (row_blocks, x_blocks))
    frob_norm = jnp.sqrt(jnp.sum(cross_products * cross_products) + 1e-06)
    polar_now = cross_products / frob_norm
    for polar_rotation_step in range(POLAR_ITER_COUNT):
        gram = jnp.dot(polar_now, polar_now.T, precision=lax.Precision.HIGHEST)
        image = jnp.dot(gram, polar_now, precision=lax.Precision.HIGHEST)
        second = jnp.dot(gram, image, precision=lax.Precision.HIGHEST)
        polar_now = quintic_one * polar_now + quintic_three * image + quintic_five * second
    return (books_now, polar_now)
```

```python
import functools

import jax
import jax.numpy as jnp
from jax import lax
from jax.experimental import pallas as pl
from jax.experimental.pallas import tpu as pltpu
from jax.sharding import PartitionSpec as P

SUB_DIM = 16
ITERS = 2
LOG2E = 1.4426950408889634
STAT_ROWS = 24

prior_weight = 8.0
quintic_one = 3.4445
quintic_three = -4.775
quintic_five = 2.0315
MESH = pl.DeviceIdType.MESH


def split_three(value):
    high = value.astype(jnp.bfloat16)
    rest = value - high.astype(jnp.float32)
    middle = rest.astype(jnp.bfloat16)
    low = (rest - middle.astype(jnp.float32)).astype(jnp.bfloat16)
    return high, middle, low


def pass_kernel(feat_ref, book_ref, stats_ref, *weights_refs):
    group, dim, rows = feat_ref.shape
    codes = book_ref.shape[2]
    chunk = 256 if rows % 256 == 0 else rows
    ones = jnp.ones((16, rows), jnp.bfloat16)
    row = lax.broadcasted_iota(jnp.int32, (16, codes), 0)
    for g in range(group):
        book = book_ref[g]
        scaled = book.astype(jnp.bfloat16).astype(jnp.float32) * (0.5 * LOG2E)
        squares = jnp.sum(book * book, axis=0, keepdims=True) * (-0.25 * LOG2E)
        one, two, three = (s.astype(jnp.float32) for s in split_three(squares))
        bias = jnp.where(row == 0, one, jnp.where(row == 1, two, jnp.where(row == 2, three, 0.0)))
        lhs = jnp.concatenate([*split_three(scaled), bias.astype(jnp.bfloat16)], axis=0)
        feat = feat_ref[g]
        rhs = jnp.concatenate([feat, feat, feat, ones], axis=0)
        feat_one = jnp.concatenate([feat, ones], axis=0)
        stats = None
        for start in range(0, rows, chunk):
            logits = lax.dot_general(
                lhs, rhs[:, start : start + chunk], (((0,), (0,)), ((), ())),
                preferred_element_type=jnp.float32,
            )
            exponent = jnp.exp2(logits - jnp.max(logits, axis=0, keepdims=True))
            inverse = 1.0 / jnp.sum(exponent, axis=0, keepdims=True)
            weights = (exponent * inverse).astype(jnp.bfloat16)
            for ref in weights_refs:
                ref[g, :, start : start + chunk] = weights
            part = lax.dot_general(
                feat_one[:, start : start + chunk], weights, (((1,), (1,)), ((), ())),
                preferred_element_type=jnp.float32,
            )
            stats = part if stats is None else stats + part
        stats_ref[g] = stats[:STAT_ROWS]


def subspace_pass(pieces, books, keep_weights):
    subs, dim, rows = pieces.shape
    codes = books.shape[2]
    group = 4 if subs % 4 == 0 else 1
    out_shape = [jax.ShapeDtypeStruct((subs, STAT_ROWS, codes), jnp.float32)]
    out_specs = [pl.BlockSpec((group, STAT_ROWS, codes), lambda i: (i, 0, 0))]
    if keep_weights:
        out_shape.append(jax.ShapeDtypeStruct((subs, codes, rows), jnp.bfloat16))
        out_specs.append(pl.BlockSpec((group, codes, rows), lambda i: (i, 0, 0)))
    return pl.pallas_call(
        pass_kernel,
        grid=(subs // group,),
        out_shape=out_shape,
        in_specs=[
            pl.BlockSpec((group, dim, rows), lambda i: (i, 0, 0)),
            pl.BlockSpec((group, dim, codes), lambda i: (i, 0, 0)),
        ],
        out_specs=out_specs,
        compiler_params=pltpu.CompilerParams(vmem_limit_bytes=32 * 2**20),
        cost_estimate=pl.CostEstimate(
            flops=subs * codes * rows * 128,
            bytes_accessed=subs * codes * rows * 2,
            transcendentals=subs * codes * rows,
        ),
    )(pieces, books)


def exchange(n, part_ref, finish, total_ref, low_ref, got_pair, low_pair, got, sems):
    pair_send, pair_recv, send, recv, out_send, out_recv, last_send, last_recv = sems
    half = n // 2
    me = lax.axis_index("rows")
    mine, side = me // 2, lax.rem(me, 2)
    sibling = me + 1 - 2 * side

    barrier = pltpu.get_barrier_semaphore()
    pl.semaphore_signal(barrier, inc=1, device_id={"rows": sibling}, device_id_type=MESH)
    for d in range(1, half):
        peer = lax.rem(mine + d, half) * 2 + side
        pl.semaphore_signal(barrier, inc=1, device_id={"rows": peer}, device_id_type=MESH)
    pl.semaphore_wait(barrier, half)

    pair = pltpu.make_async_remote_copy(
        src_ref=part_ref.at[:, 1 - side], dst_ref=got_pair, send_sem=pair_send, recv_sem=pair_recv,
        device_id={"rows": sibling}, device_id_type=MESH,
    )
    pair.start()
    pair.wait()

    copies = []
    for d in range(1, half):
        spot = lax.rem(mine + d, half)
        summed = part_ref[spot, side].astype(jnp.float32) + got_pair[spot].astype(jnp.float32)
        low_pair[spot] = summed.astype(low_pair.dtype)
        copy = pltpu.make_async_remote_copy(
            src_ref=low_pair.at[spot], dst_ref=got.at[d], send_sem=send.at[d], recv_sem=recv.at[d],
            device_id={"rows": spot * 2 + side}, device_id_type=MESH,
        )
        copy.start()
        copies.append(copy)
    total = part_ref[mine, side].astype(jnp.float32) + got_pair[mine].astype(jnp.float32)
    for d in range(1, half):
        copies[d - 1].wait_recv()
        total += got[d].astype(jnp.float32)
    result = finish(total)
    if total_ref is not None:
        total_ref[...] = result
    low_ref[mine, side] = result.astype(low_ref.dtype)

    outs = []
    for d in range(1, half):
        spot = lax.rem(mine + d, half)
        copy = pltpu.make_async_remote_copy(
            src_ref=low_ref.at[mine, side], dst_ref=low_ref.at[mine, side],
            send_sem=out_send.at[d], recv_sem=out_recv.at[d],
            device_id={"rows": spot * 2 + side}, device_id_type=MESH,
        )
        copy.start()
        outs.append(copy)
    for copy in copies:
        copy.wait_send()
    for copy in outs:
        copy.wait()
    last = pltpu.make_async_remote_copy(
        src_ref=low_ref.at[:, side], dst_ref=low_ref.at[:, side],
        send_sem=last_send, recv_sem=last_recv, device_id={"rows": sibling}, device_id_type=MESH,
    )
    last.start()
    last.wait()


def books_kernel(n, part_ref, old_ref, new_ref, got_pair, low_pair, got, *sems):
    me = lax.axis_index("rows")
    old = old_ref[me // 2, lax.rem(me, 2)]

    def finish(total):
        top = total[:, :SUB_DIM] + prior_weight * old
        return top / (total[:, SUB_DIM : SUB_DIM + 1] + prior_weight)

    exchange(n, part_ref, finish, None, new_ref, got_pair, low_pair, got, sems)


def cross_kernel(n, part_ref, total_ref, low_ref, got_pair, low_pair, got, *sems):
    exchange(n, part_ref, lambda total: total, total_ref, low_ref, got_pair, low_pair, got, sems)


def scratch(n, piece, dtype):
    half = n // 2
    one, many = pltpu.SemaphoreType.DMA, pltpu.SemaphoreType.DMA((half,))
    return [pltpu.VMEM((half, *piece), dtype)] * 3 + [one, one, many, many, many, many, one, one]


def whole_in_vmem(count):
    return [pl.BlockSpec(memory_space=pltpu.VMEM)] * count


def update_books(n, stats, books, collective_id):
    subs, dim, codes = books.shape
    if n % 2 or subs % n:
        stats = lax.psum(stats, "rows")
        top = stats[:, :SUB_DIM] + prior_weight * books
        return top / (stats[:, SUB_DIM : SUB_DIM + 1] + prior_weight)
    own = subs // n
    return pl.pallas_call(
        functools.partial(books_kernel, n),
        out_shape=jax.ShapeDtypeStruct((n // 2, 2, own, dim, codes), jnp.float32),
        in_specs=whole_in_vmem(2),
        out_specs=whole_in_vmem(1)[0],
        scratch_shapes=scratch(n, (own, STAT_ROWS, codes), jnp.float32),
        compiler_params=pltpu.CompilerParams(
            collective_id=collective_id, has_side_effects=True, vmem_limit_bytes=32 * 2**20
        ),
    )(
        stats.reshape(n // 2, 2, own, STAT_ROWS, codes), books.reshape(n // 2, 2, own, dim, codes)
    ).reshape(books.shape)


def sum_cross(n, partial, collective_id):
    height, width = partial.shape
    own = height // n
    total, low = pl.pallas_call(
        functools.partial(cross_kernel, n),
        out_shape=[
            jax.ShapeDtypeStruct((own, width), jnp.float32),
            jax.ShapeDtypeStruct((n // 2, 2, own, width), jnp.bfloat16),
        ],
        in_specs=whole_in_vmem(1),
        out_specs=whole_in_vmem(2),
        scratch_shapes=scratch(n, (own, width), jnp.bfloat16),
        compiler_params=pltpu.CompilerParams(
            collective_id=collective_id, has_side_effects=True, vmem_limit_bytes=32 * 2**20
        ),
    )(partial.reshape(n // 2, 2, own, width))
    return total, low.reshape(height, width)


def product(a, b, b_side=0):
    return lax.dot_general(
        a.astype(jnp.bfloat16), b, (((1,), (b_side,)), ((), ())), preferred_element_type=jnp.float32
    )


def per_device(n, n_sub, embeddings, rotation, codebooks):
    def over_sub(value):
        return lax.psum(value, "sub") if n_sub > 1 else value

    row_count = embeddings.shape[0]
    width = rotation.shape[1]
    subs = codebooks.shape[0]
    full_x = embeddings
    if n_sub > 1:
        full_x = lax.all_gather(embeddings, "sub", axis=1, tiled=True)
    rotated = lax.dot_general(
        rotation, full_x, (((0,), (1,)), ((), ())), preferred_element_type=jnp.float32
    ).astype(jnp.bfloat16)
    pieces = rotated.reshape(subs, SUB_DIM, row_count)
    books = codebooks
    for repeat in range(ITERS):
        stats, *weights = subspace_pass(pieces, books, repeat == ITERS - 1)
        books = update_books(n, stats, books, repeat)
    rebuilt = jnp.einsum(
        "mdk,mkr->mdr", books.astype(jnp.bfloat16), weights[0], preferred_element_type=jnp.float32
    )
    rebuilt = rebuilt.reshape(width, row_count).astype(jnp.bfloat16)
    partial = lax.dot_general(
        full_x, rebuilt, (((0,), (1,)), ((), ())), preferred_element_type=jnp.float32
    ).astype(jnp.bfloat16)
    own, low = sum_cross(n, partial, ITERS)

    wide = low.astype(jnp.float32)
    inverse = lax.rsqrt(over_sub(jnp.sum(wide * wide)) + 1e-06)
    gram = (over_sub(product(low, low, 1)) * (inverse * inverse)).astype(jnp.bfloat16)
    image = product(gram, low) * inverse
    second = product(gram, image.astype(jnp.bfloat16))
    change = quintic_three * image + quintic_five * second
    polar = (quintic_one * inverse * wide + change).astype(jnp.bfloat16)
    own_height = own.shape[0]
    own_change = lax.dynamic_slice_in_dim(change, lax.axis_index("rows") * own_height, own_height, 0)
    own = quintic_one * inverse * own + own_change

    gram_rows = over_sub(product(own, polar, 1))
    image_rows = product(gram_rows, polar)
    second_rows = product(over_sub(product(image_rows, polar, 1)), polar)
    own = quintic_one * own + quintic_three * image_rows + quintic_five * second_rows
    return (books, own)


def solution(mesh):
    return jax.shard_map(
        functools.partial(per_device, mesh.shape["rows"], mesh.shape["sub"]),
        mesh=mesh,
        in_specs=(P("rows", "sub"), P(None, "sub"), P("sub", None, None)),
        out_specs=(P("sub", None, None), P("rows", "sub")),
        check_vma=False,
    )
```

```python
import functools

import jax
import jax.numpy as jnp
from jax import lax
from jax.experimental import pallas as pl
from jax.experimental.pallas import tpu as pltpu
from jax.sharding import PartitionSpec as P

SUB_DIM = 16
ITERS = 2
LOG2E = 1.4426950408889634

prior_weight = 8.0
quintic_one = 3.4445
quintic_three = -4.775
quintic_five = 2.0315
MESH = pl.DeviceIdType.MESH


def split_three(value):
    high = value.astype(jnp.bfloat16)
    rest = value - high.astype(jnp.float32)
    middle = rest.astype(jnp.bfloat16)
    low = (rest - middle.astype(jnp.float32)).astype(jnp.bfloat16)
    return high, middle, low


def pass_kernel(own, packed, feat_ref, book_ref, stats_ref, *weights_refs):
    group, dim, rows = feat_ref.shape
    codes = book_ref.shape[2]
    chunk = 256 if rows % 256 == 0 else rows
    ones = jnp.ones((16, rows), jnp.bfloat16)
    row = lax.broadcasted_iota(jnp.int32, (16, codes), 0)
    for g in range(group):
        piece, spot = g // own, g % own
        if packed:
            low = book_ref[piece, spot * dim : spot * dim + dim]
            tile = book_ref[piece, own * dim :].astype(jnp.float32)
            bias = jnp.where((row >= 3 * spot) & (row < 3 * spot + 3), tile, 0.0)
        else:
            low = book_ref[g].astype(jnp.bfloat16)
            bias = square_rows(row, 0, book_ref[g], 0.0)
        scaled = low.astype(jnp.float32) * (0.5 * LOG2E)
        lhs = jnp.concatenate([*split_three(scaled), bias.astype(jnp.bfloat16)], axis=0)
        feat = feat_ref[g]
        rhs = jnp.concatenate([feat, feat, feat, ones], axis=0)
        feat_one = jnp.concatenate([feat, ones], axis=0)
        stats = None
        for start in range(0, rows, chunk):
            logits = lax.dot_general(
                lhs, rhs[:, start : start + chunk], (((0,), (0,)), ((), ())),
                preferred_element_type=jnp.float32,
            )
            exponent = jnp.exp2(logits - jnp.max(logits, axis=0, keepdims=True))
            inverse = 1.0 / jnp.sum(exponent, axis=0, keepdims=True)
            weights = (exponent * inverse).astype(jnp.bfloat16)
            for ref in weights_refs:
                ref[g, :, start : start + chunk] = weights
            part = lax.dot_general(
                feat_one[:, start : start + chunk], weights, (((1,), (1,)), ((), ())),
                preferred_element_type=jnp.float32,
            )
            stats = part if stats is None else stats + part
        stats_ref[piece, spot * dim : spot * dim + dim] = stats[:dim]
        counts = jnp.where(row == spot, stats[dim:], 0.0 if spot == 0 else counts)
        if spot == own - 1:
            stats_ref[piece, own * dim :] = counts


def square_rows(row, spot, book, others):
    squares = jnp.sum(book * book, axis=0, keepdims=True) * (-0.25 * LOG2E)
    for k, term in enumerate(split_three(squares)):
        others = jnp.where(row == 3 * spot + k, term.astype(jnp.float32), others)
    return others


def subspace_pass(own, pieces, books, keep_weights):
    subs, dim, rows = pieces.shape
    packed = books.dtype == jnp.bfloat16
    codes = books.shape[2]
    group = max(own, 4 if subs % 4 == 0 else 1)
    height = own * dim + 16
    out_shape = [jax.ShapeDtypeStruct((subs // own, height, codes), jnp.float32)]
    out_specs = [pl.BlockSpec((group // own, height, codes), lambda i: (i, 0, 0))]
    if keep_weights:
        out_shape.append(jax.ShapeDtypeStruct((subs, codes, rows), jnp.bfloat16))
        out_specs.append(pl.BlockSpec((group, codes, rows), lambda i: (i, 0, 0)))
    book_block = (group // own, height, codes) if packed else (group, dim, codes)
    return pl.pallas_call(
        functools.partial(pass_kernel, own, packed),
        grid=(subs // group,),
        out_shape=out_shape,
        in_specs=[
            pl.BlockSpec((group, dim, rows), lambda i: (i, 0, 0)),
            pl.BlockSpec(book_block, lambda i: (i, 0, 0)),
        ],
        out_specs=out_specs,
        compiler_params=pltpu.CompilerParams(vmem_limit_bytes=32 * 2**20),
        cost_estimate=pl.CostEstimate(
            flops=subs * codes * rows * 128,
            bytes_accessed=subs * codes * rows * 2,
            transcendentals=subs * codes * rows,
        ),
    )(pieces, books)


def exchange(n, part_ref, finish, total_ref, low_ref, buffers, sems):
    got_pair, low_pair, got, *sent_pair = buffers
    pair_send, pair_recv, send, recv, out_send, out_recv, last_send, last_recv = sems
    half = n // 2
    me = lax.axis_index("rows")
    mine, side = me // 2, lax.rem(me, 2)
    sibling = me + 1 - 2 * side

    barrier = pltpu.get_barrier_semaphore()
    pl.semaphore_signal(barrier, inc=1, device_id={"rows": sibling}, device_id_type=MESH)
    for d in range(1, half):
        peer = lax.rem(mine + d, half) * 2 + side
        pl.semaphore_signal(barrier, inc=1, device_id={"rows": peer}, device_id_type=MESH)
    if sent_pair:
        for spot in range(half):
            sent_pair[0][spot] = part_ref[spot, 1 - side].astype(jnp.bfloat16)
        pair_source = sent_pair[0]
    else:
        pair_source = part_ref.at[:, 1 - side]
    pl.semaphore_wait(barrier, half)

    pair = pltpu.make_async_remote_copy(
        src_ref=pair_source, dst_ref=got_pair, send_sem=pair_send, recv_sem=pair_recv,
        device_id={"rows": sibling}, device_id_type=MESH,
    )
    pair.start()
    pair.wait()

    copies = []
    for d in range(1, half):
        spot = lax.rem(mine + d, half)
        summed = part_ref[spot, side].astype(jnp.float32) + got_pair[spot].astype(jnp.float32)
        low_pair[spot] = summed.astype(low_pair.dtype)
        copy = pltpu.make_async_remote_copy(
            src_ref=low_pair.at[spot], dst_ref=got.at[d], send_sem=send.at[d], recv_sem=recv.at[d],
            device_id={"rows": spot * 2 + side}, device_id_type=MESH,
        )
        copy.start()
        copies.append(copy)
    total = part_ref[mine, side].astype(jnp.float32) + got_pair[mine].astype(jnp.float32)
    for d in range(1, half):
        copies[d - 1].wait_recv()
        total += got[d].astype(jnp.float32)
    kept, shared = finish(total)
    total_ref[...] = kept
    low_ref[mine, side] = shared

    outs = []
    for d in range(1, half):
        spot = lax.rem(mine + d, half)
        copy = pltpu.make_async_remote_copy(
            src_ref=low_ref.at[mine, side], dst_ref=low_ref.at[mine, side],
            send_sem=out_send.at[d], recv_sem=out_recv.at[d],
            device_id={"rows": spot * 2 + side}, device_id_type=MESH,
        )
        copy.start()
        outs.append(copy)
    for copy in copies:
        copy.wait_send()
    for copy in outs:
        copy.wait()
    last = pltpu.make_async_remote_copy(
        src_ref=low_ref.at[:, side], dst_ref=low_ref.at[:, side],
        send_sem=last_send, recv_sem=last_recv, device_id={"rows": sibling}, device_id_type=MESH,
    )
    last.start()
    last.wait()


def books_kernel(n, part_ref, old_ref, new_ref, low_ref, *rest):
    own, dim, codes = old_ref.shape
    row = lax.broadcasted_iota(jnp.int32, (16, codes), 0)

    def finish(total):
        kept, bias = [], 0.0
        for spot in range(own):
            top = total[spot * dim : spot * dim + dim] + prior_weight * old_ref[spot]
            count = total[own * dim + spot : own * dim + spot + 1]
            kept.append(top / (count + prior_weight))
            bias = square_rows(row, spot, kept[spot], bias)
        shared = kept if low_ref.shape[2] == own * dim else kept + [bias]
        low = jnp.concatenate([part.astype(jnp.bfloat16) for part in shared], axis=0)
        return jnp.stack(kept), low

    exchange(n, part_ref, finish, new_ref, low_ref, rest[:4], rest[4:])


def cross_kernel(n, part_ref, total_ref, low_ref, *rest):
    def finish(total):
        return total, total.astype(jnp.bfloat16)

    exchange(n, part_ref, finish, total_ref, low_ref, rest[:3], rest[3:])


def scratch(n, piece, buffers):
    half = n // 2
    one, many = pltpu.SemaphoreType.DMA, pltpu.SemaphoreType.DMA((half,))
    slots = [pltpu.VMEM((half, *piece), jnp.bfloat16)] * buffers
    return slots + [one, one, many, many, many, many, one, one]


def whole_in_vmem(count):
    return [pl.BlockSpec(memory_space=pltpu.VMEM)] * count


def update_books(n, stats, old, last, collective_id):
    own, dim, codes = old.shape
    height = stats.shape[1]
    kept = own * dim if last else height
    new, low = pl.pallas_call(
        functools.partial(books_kernel, n),
        out_shape=[
            jax.ShapeDtypeStruct(old.shape, jnp.float32),
            jax.ShapeDtypeStruct((n // 2, 2, kept, codes), jnp.bfloat16),
        ],
        in_specs=whole_in_vmem(2),
        out_specs=whole_in_vmem(2),
        scratch_shapes=scratch(n, (height, codes), 4),
        compiler_params=pltpu.CompilerParams(
            collective_id=collective_id, has_side_effects=True, vmem_limit_bytes=32 * 2**20
        ),
    )(stats.reshape(n // 2, 2, height, codes), old)
    return new, low.reshape(n, kept, codes)


def sum_cross(n, partial, collective_id):
    height, width = partial.shape
    own = height // n
    total, low = pl.pallas_call(
        functools.partial(cross_kernel, n),
        out_shape=[
            jax.ShapeDtypeStruct((own, width), jnp.float32),
            jax.ShapeDtypeStruct((n // 2, 2, own, width), jnp.bfloat16),
        ],
        in_specs=whole_in_vmem(1),
        out_specs=whole_in_vmem(2),
        scratch_shapes=scratch(n, (own, width), 3),
        compiler_params=pltpu.CompilerParams(
            collective_id=collective_id, has_side_effects=True, vmem_limit_bytes=32 * 2**20
        ),
    )(partial.reshape(n // 2, 2, own, width))
    return total, low.reshape(height, width)


def polar_kernel(own_ref, low_ref, out_ref, gram_ref, image_ref, change_ref, polar_ref):
    size = low_ref.shape[0]
    own_height = own_ref.shape[0]
    tile = 256 if size % 256 == 0 else size
    tiles = size // tile

    def rows(i):
        return pl.ds(pl.multiple_of(i * tile, tile), tile)

    def square(i, total):
        wide = low_ref[rows(i)].astype(jnp.float32)
        return total + jnp.sum(wide * wide, axis=0, keepdims=True)

    squares = lax.fori_loop(0, tiles, square, jnp.zeros((1, low_ref.shape[1]), jnp.float32))
    inverse = lax.rsqrt(jnp.sum(squares, axis=1, keepdims=True) + 1e-06)

    @pl.loop(0, tiles)
    def _(i):
        gram = product(low_ref[rows(i)], low_ref[...], 1) * (inverse * inverse)
        gram_ref[rows(i)] = gram.astype(jnp.bfloat16)

    @pl.loop(0, tiles)
    def _(i):
        image = product(gram_ref[rows(i)], low_ref[...]) * inverse
        image_ref[rows(i)] = image.astype(jnp.bfloat16)
        change_ref[rows(i)] = quintic_three * image

    @pl.loop(0, tiles)
    def _(i):
        change = change_ref[rows(i)] + quintic_five * product(gram_ref[rows(i)], image_ref[...])
        change_ref[rows(i)] = change
        polar = quintic_one * inverse * low_ref[rows(i)].astype(jnp.float32) + change
        polar_ref[rows(i)] = polar.astype(jnp.bfloat16)

    start = pl.multiple_of(lax.axis_index("rows") * own_height, own_height)
    own = quintic_one * inverse * own_ref[...] + change_ref[pl.ds(start, own_height)]
    image = product(product(own, polar_ref[...], 1), polar_ref[...])
    second = product(product(image, polar_ref[...], 1), polar_ref[...])
    out_ref[...] = quintic_one * own + quintic_three * image + quintic_five * second


def polar_steps(own, low):
    size, width = low.shape
    return pl.pallas_call(
        polar_kernel,
        out_shape=jax.ShapeDtypeStruct(own.shape, jnp.float32),
        in_specs=whole_in_vmem(2),
        out_specs=whole_in_vmem(1)[0],
        scratch_shapes=[
            pltpu.VMEM((size, size), jnp.bfloat16),
            pltpu.VMEM((size, width), jnp.bfloat16),
            pltpu.VMEM((size, width), jnp.float32),
            pltpu.VMEM((size, width), jnp.bfloat16),
        ],
        compiler_params=pltpu.CompilerParams(vmem_limit_bytes=40 * 2**20),
    )(own, low)


def product(a, b, b_side=0):
    return lax.dot_general(
        a.astype(jnp.bfloat16), b.astype(jnp.bfloat16), (((1,), (b_side,)), ((), ())), preferred_element_type=jnp.float32
    )


def per_device(n, n_sub, embeddings, rotation, codebooks):
    def over_sub(value):
        return lax.psum(value, "sub") if n_sub > 1 else value

    row_count = embeddings.shape[0]
    width = rotation.shape[1]
    subs = codebooks.shape[0]
    full_x = embeddings
    if n_sub > 1:
        full_x = lax.all_gather(embeddings, "sub", axis=1, tiled=True)
    rotated = lax.dot_general(
        rotation, full_x, (((0,), (1,)), ((), ())), preferred_element_type=jnp.float32
    ).astype(jnp.bfloat16)
    pieces = rotated.reshape(subs, SUB_DIM, row_count)
    split_books = n % 2 == 0 and subs % n == 0 and 3 * (subs // n) <= 16
    own_subs = subs // n if split_books else 1
    books, own = codebooks, codebooks
    if split_books:
        own = lax.dynamic_slice_in_dim(codebooks, lax.axis_index("rows") * own_subs, own_subs, 0)
    for repeat in range(ITERS):
        last = repeat == ITERS - 1
        stats, *weights = subspace_pass(own_subs, pieces, books, last)
        if split_books:
            own, books = update_books(n, stats, own, last, repeat)
        else:
            stats = lax.psum(stats, "rows")
            top = stats[:, :SUB_DIM] + prior_weight * books
            books = top / (stats[:, SUB_DIM : SUB_DIM + 1] + prior_weight)
    books = books.reshape(codebooks.shape)
    rebuilt = jnp.einsum(
        "mdk,mkr->mdr", books.astype(jnp.bfloat16), weights[0], preferred_element_type=jnp.float32
    )
    books = books.astype(jnp.float32)
    rebuilt = rebuilt.reshape(width, row_count).astype(jnp.bfloat16)
    partial = lax.dot_general(
        full_x, rebuilt, (((0,), (1,)), ((), ())), preferred_element_type=jnp.float32
    ).astype(jnp.bfloat16)
    own, low = sum_cross(n, partial, ITERS)
    if n_sub == 1:
        return (books, polar_steps(own, low))

    wide = low.astype(jnp.float32)
    inverse = lax.rsqrt(over_sub(jnp.sum(wide * wide)) + 1e-06)
    gram = (over_sub(product(low, low, 1)) * (inverse * inverse)).astype(jnp.bfloat16)
    image = product(gram, low) * inverse
    second = product(gram, image.astype(jnp.bfloat16))
    change = quintic_three * image + quintic_five * second
    polar = (quintic_one * inverse * wide + change).astype(jnp.bfloat16)
    own_height = own.shape[0]
    own_change = lax.dynamic_slice_in_dim(change, lax.axis_index("rows") * own_height, own_height, 0)
    own = quintic_one * inverse * own + own_change

    gram_rows = over_sub(product(own, polar, 1))
    image_rows = product(gram_rows, polar)
    second_rows = product(over_sub(product(image_rows, polar, 1)), polar)
    own = quintic_one * own + quintic_three * image_rows + quintic_five * second_rows
    return (books, own)


def solution(mesh):
    return jax.shard_map(
        functools.partial(per_device, mesh.shape["rows"], mesh.shape["sub"]),
        mesh=mesh,
        in_specs=(P("rows", "sub"), P(None, "sub"), P("sub", None, None)),
        out_specs=(P("sub", None, None), P("rows", "sub")),
        check_vma=False,
    )
```
